256 devices in a mesh: replica: 32 (over x, z), tensor: 8 (over y, core).
Axes of the slice: x: 4, y: 4, z: 8, core: 2. Of those that a mesh axis runs over, the one named last changes fastest.
Arguments:
- ssm_state: bfloat16 [128, 128, 4096], P('replica', None, 'tensor'), may hold values from -6 to 6
- kcache: bfloat16 [128, 1024, 1024], P('replica', None, 'tensor'), may hold values from -6 to 6
- vcache: bfloat16 [128, 1024, 1024], P('replica', None, 'tensor'), may hold values from -6 to 6
- lengths: int32 [32], replicated, may hold values from 128 to 1024, as said below
- parents: int32 [2, 128], replicated, may hold values from 0 to 127, as said below
- x_in: bfloat16 [2, 128, 4096], P(None, 'replica', 'tensor'), may hold values from -6 to 6
- z_in: bfloat16 [2, 128, 4096], P(None, 'replica', 'tensor'), may hold values from -6 to 6
- dt_in: bfloat16 [2, 128, 64], P(None, 'replica', 'tensor'), may hold values from -4 to 4
- b_in: bfloat16 [2, 128, 128], P(None, 'replica'), may hold values from -0.5 to 0.5
- c_in: bfloat16 [2, 128, 128], P(None, 'replica'), may hold values from -0.5 to 0.5
- q_in: bfloat16 [2, 128, 8192], P(None, 'replica', 'tensor'), may hold values from -100 to 100
- kv_new: bfloat16 [2, 128, 2, 1024], P(None, 'replica', None, 'tensor'), may hold values from -12 to 12
- a_rate: float32 [64], P('tensor'), may hold values from 0.05 to 8
- dt_bias: float32 [64], P('tensor'), may hold values from -3 to 0
- skip: float32 [64], P('tensor'), may hold values from 0.5 to 1.5
- gain: float32 [4096], P('tensor'), may hold values from 0.5 to 1.5
- out_proj: bfloat16 [4096, 4096], P('tensor'), may hold values from -0.09375 to 0.09375
Outputs:
- final_state: bfloat16 [128, 128, 4096], P('replica', None, 'tensor')
- mamba_out: bfloat16 [2, 128, 4096], P(None, 'replica', 'tensor')
- attn_out: bfloat16 [2, 128, 8192], P(None, 'replica', 'tensor')
The draws below stay inside these ranges and needn't reach their ends.
Inputs may be any that keep to these rules, and one draw needn't show every extreme that they name: In each step the 4 slots of a prompt take their parents among the 4 slots of one prompt, and each prompt is that source for exactly one prompt. `lengths`: multiples of 128; some prompt's cache is full.
All inputs are finite; a program needn't handle non-finite values.
Results may differ from the reference program's by a relative error of at most 0.019.
Values may be sent and summed in bfloat16 or wider, within the bound.
No kernel may reach another device: no remote copies, remote signals or barrier semaphores. Data moves between devices by JAX's collectives and lax.ppermute only.
A program may use at most 64 MiB of HBM per device.

```python
import math
import jax
import jax.numpy as jnp
from jax import lax

D = 4096
HEADS = 64
HEAD = 64
STATE = 128
NORM_GROUP = 512
Q_HEADS = 64
KV_HEADS = 8
HD = 128
BEAM = 4
PAGE = 128
CACHE = 1024
SLOTS = 128
PROMPTS = 32


def draw_kcache(key, part):
    key = jax.random.fold_in(key, 9)
    shape = (SLOTS, CACHE, KV_HEADS, HD)
    noise = jnp.clip(jax.random.normal(key, shape, jnp.float32), -6.0, 6.0)
    return noise.reshape(SLOTS, CACHE, KV_HEADS * HD).astype(jnp.bfloat16)


def draw_q_in(key, part):
    key = jax.random.fold_in(key, 7)
    shape = (2, SLOTS, Q_HEADS, HD)
    noise = jnp.clip(1.5 * jax.random.normal(key, shape, jnp.float32), -9.0, 9.0)
    return noise.reshape(2, SLOTS, Q_HEADS * HD).astype(jnp.bfloat16)


def draw_parents(key, part):
    key = jax.random.fold_in(key, 3)
    rounds = []
    for step_id in range(2):
        step_key = jax.random.fold_in(key, step_id)
        order = jax.random.permutation(jax.random.fold_in(step_key, 1), PROMPTS)
        picked_beams = jax.random.randint(jax.random.fold_in(step_key, 2), (PROMPTS, BEAM), 0, BEAM)
        rounds.append((order[:, None] * BEAM + picked_beams).reshape(-1))
    return jnp.stack(rounds).astype(jnp.int32)


def draw_lengths(key, part):
    key = jax.random.fold_in(key, 5)
    pages = jax.random.randint(key, (PROMPTS,), 1, CACHE // PAGE + 1)
    full_at = jax.random.randint(jax.random.fold_in(key, 1), (), 0, PROMPTS)
    pages = jnp.where(jnp.arange(PROMPTS) == full_at, CACHE // PAGE, pages)
    return (pages * PAGE).astype(jnp.int32)


def block_levels(own_key, shape, pieces, least, top_value):
    loudness = 1.0
    for axis_at, parts in pieces:
        heights = jax.random.uniform(jax.random.fold_in(jax.random.fold_in(own_key, 6), axis_at), (parts,), jnp.float32, least / len(pieces), top_value / len(pieces))
        loudness = loudness * jnp.repeat(jnp.exp(heights), shape[axis_at] // parts).reshape((-1,) + (1,) * (len(shape) - 1 - axis_at))
    return loudness


def centred(stream_key, extent, scale, most, shards=(), kind=jnp.bfloat16):
    result = jax.random.normal(stream_key, extent, jnp.float32) * scale
    if len(shards) > 0:
        result = block_levels(stream_key, extent, shards, -0.22, 0.18) * result
    return jnp.clip(result, min=-most, max=most).astype(kind)


def setup_inputs(seed: int = 0) -> dict:
    arg_keys = jax.random.split(jax.random.key(seed), 18)
    return {
        "ssm_state": centred(arg_keys[0], (SLOTS, STATE, HEADS * HEAD), 1.0, 6.0, ((0, 32), (2, 8))),
        "kcache": draw_kcache(jax.random.fold_in(arg_keys[17], 71), 0),
        "vcache": centred(arg_keys[2], (SLOTS, CACHE, KV_HEADS * HD), 1.0, 6.0, ((0, 32), (2, 8))),
        "lengths": draw_lengths(jax.random.fold_in(arg_keys[17], 71), 0),
        "parents": draw_parents(jax.random.fold_in(arg_keys[17], 71), 0),
        "x_in": centred(arg_keys[5], (2, SLOTS, HEADS * HEAD), 1.0, 6.0, ((1, 32), (2, 8))),
        "z_in": centred(arg_keys[6], (2, SLOTS, HEADS * HEAD), 1.0, 6.0, ((1, 32), (2, 8))),
        "dt_in": centred(arg_keys[7], (2, SLOTS, HEADS), 1.0, 4.0, ((1, 32), (2, 8))),
        "b_in": centred(arg_keys[8], (2, SLOTS, STATE), STATE ** -0.5, 0.5, ((1, 32),)),
        "c_in": centred(arg_keys[9], (2, SLOTS, STATE), STATE ** -0.5, 0.5, ((1, 32),)),
        "q_in": draw_q_in(jax.random.fold_in(arg_keys[17], 71), 0),
        "kv_new": centred(arg_keys[11], (2, SLOTS, 2, KV_HEADS * HD), 2.0, 12.0, ((1, 32), (3, 8))),
        "a_rate": jnp.clip(jnp.exp(math.log(8.0) - 5.075174 * jax.random.uniform(arg_keys[12], (HEADS,), jnp.float32) ** block_levels(arg_keys[12], (HEADS,), ((0, 8),), -0.2, 0.2)), 0.05, 8.0),
        "dt_bias": jnp.clip(-3.0 + 3.0 * jax.random.uniform(arg_keys[13], (HEADS,), jnp.float32) ** block_levels(arg_keys[13], (HEADS,), ((0, 8),), -0.2, 0.2), -3.0, 0.0),
        "skip": jnp.clip(0.5 + 1.0 * jax.random.uniform(arg_keys[14], (HEADS,), jnp.float32) ** block_levels(arg_keys[14], (HEADS,), ((0, 8),), -0.2, 0.2), 0.5, 1.5),
        "gain": jnp.clip(1.0 + 0.1 * jax.random.normal(arg_keys[15], (HEADS * HEAD,), jnp.float32), 0.5, 1.5),
        "out_proj": centred(arg_keys[16], (HEADS * HEAD, D), (HEADS * HEAD) ** -0.5, 0.09375, ((0, 8),)),
    }


MASKED = -1e+30

def ssm_advance(carried, x_row, z_row, dt_row, b_row, c_row, a_rate, dt_bias, skip, gain):
    row_count = carried.shape[0]
    step_size = jax.nn.softplus(dt_row.astype(jnp.float32) + dt_bias)
    decay_rate = jnp.repeat(jnp.exp(-a_rate * step_size), HEAD, axis=1)
    drive_term = jnp.repeat(step_size, HEAD, axis=1) * x_row.astype(jnp.float32)
    updated = decay_rate[:, None, :] * carried.astype(jnp.float32) + drive_term[:, None, :] * b_row.astype(jnp.float32)[:, :, None]
    ssm_out = lax.optimization_barrier(jnp.sum(updated * c_row.astype(jnp.float32)[:, :, None], axis=1)) + jnp.repeat(skip, HEAD) * x_row.astype(jnp.float32)
    gated_out = ssm_out * jax.nn.silu(z_row.astype(jnp.float32))
    grouped = gated_out.reshape(row_count, -1, NORM_GROUP)
    scaled = grouped * lax.rsqrt(lax.optimization_barrier(jnp.mean(grouped * grouped, axis=-1, keepdims=True)) + 1e-05)
    normed = (scaled.reshape(row_count, -1) * gain).astype(jnp.bfloat16)
    return (updated.astype(jnp.bfloat16), normed)

def attend_one(query, key_block, value_block, cap_len, extra_keys, extra_values):
    group_size = Q_HEADS // KV_HEADS
    query_view = query.astype(jnp.float32).reshape(KV_HEADS, group_size, HD)
    all_keys = jnp.concatenate([key_block, extra_keys], axis=0).astype(jnp.float32).reshape(-1, KV_HEADS, HD)
    all_values = jnp.concatenate([value_block, extra_values], axis=0).astype(jnp.float32).reshape(-1, KV_HEADS, HD)
    scores = jnp.einsum('kgd,nkd->kgn', query_view, all_keys, precision=lax.Precision.HIGHEST) * HD ** (-0.5)
    positions = jnp.arange(all_keys.shape[0], dtype=jnp.int32)
    live_mask = (positions < cap_len) | (positions >= CACHE)
    scores = jnp.where(live_mask, scores, MASKED)
    row_max = lax.optimization_barrier(jnp.max(scores, axis=-1, keepdims=True))
    weights = jnp.where(live_mask, jnp.exp(scores - row_max), 0.0)
    weight_sum = lax.optimization_barrier(jnp.sum(weights, axis=-1))
    rounded = lax.optimization_barrier(weights.astype(jnp.bfloat16)).astype(jnp.float32)
    mixture = jnp.einsum('kgn,nkd->kgd', rounded, all_values, precision=lax.Precision.HIGHEST)
    return (mixture / weight_sum[..., None]).reshape(-1).astype(jnp.bfloat16)

def reference(ssm_state, kcache, vcache, lengths, parents, x_in, z_in, dt_in, b_in, c_in, q_in, kv_new, a_rate, dt_bias, skip, gain, out_proj):
    carried = ssm_state
    projected = []
    for step_id in range(2):
        carried, normed = ssm_advance(carried[parents[step_id]], x_in[step_id], z_in[step_id], dt_in[step_id], b_in[step_id], c_in[step_id], a_rate, dt_bias, skip, gain)
        projected.append(jnp.dot(normed, out_proj, preferred_element_type=jnp.float32).astype(jnp.bfloat16))
    first_parents = parents[0]
    second_parents = parents[1]

    def first_slot(slot_id):
        root = first_parents[slot_id]
        cap_len = lengths[root // BEAM]
        return attend_one(q_in[0, slot_id], kcache[root], vcache[root], cap_len, kv_new[0, slot_id, 0][None], kv_new[0, slot_id, 1][None])

    def second_slot(slot_id):
        parent = second_parents[slot_id]
        root = first_parents[parent]
        cap_len = lengths[root // BEAM]
        extra_keys = jnp.stack([kv_new[0, parent, 0], kv_new[1, slot_id, 0]])
        extra_values = jnp.stack([kv_new[0, parent, 1], kv_new[1, slot_id, 1]])
        return attend_one(q_in[1, slot_id], kcache[root], vcache[root], cap_len, extra_keys, extra_values)
    slot_ids = jnp.arange(SLOTS, dtype=jnp.int32)
    attended = jnp.stack([lax.map(first_slot, slot_ids), lax.map(second_slot, slot_ids)])
    return (carried, jnp.stack(projected), attended)
```

```python
import functools

import jax
import jax.numpy as jnp
from jax import lax
from jax.experimental import pallas as pl
from jax.experimental.pallas import tpu as pltpu
from jax.sharding import PartitionSpec as P

F32 = jnp.float32
BF16 = jnp.bfloat16
HD = 128
STEP_LANES = 1408
CARRY_LANES = 384
ITEM_LANES = STEP_LANES + CARRY_LANES
BACK_LANES = 1536
MASKED = -1e30
VMEM_LIMIT = 40 * 1024 * 1024

SMEM = pl.BlockSpec(memory_space=pltpu.SMEM)
VMEM = pl.BlockSpec(memory_space=pltpu.VMEM)


def call(body, name, out_shape, in_specs, out_specs, scratch=(), cost=(1000000, 1000000)):
    return pl.pallas_call(
        body,
        name=name,
        out_shape=out_shape,
        in_specs=in_specs,
        out_specs=out_specs,
        scratch_shapes=list(scratch),
        compiler_params=pltpu.CompilerParams(vmem_limit_bytes=VMEM_LIMIT),
        cost_estimate=pl.CostEstimate(flops=cost[0], bytes_accessed=cost[1], transcendentals=0),
    )


def source_of(parents, step, prompt):
    return parents[step, prompt * 4] >> 2


def root_of(parents, prompt):
    return source_of(parents, 0, source_of(parents, 1, prompt))


def pack_body(parents, q, kv, c, x, b, dt, item, inverse, wide):
    def fill(prompt, _):
        inverse[0, source_of(parents, 0, prompt)] = prompt
        inverse[1, root_of(parents, prompt)] = prompt
        return 0

    lax.fori_loop(0, 32, fill, 0)
    wide[:, STEP_LANES:] = jnp.zeros((8, CARRY_LANES), F32)
    for t in range(2):
        rows = pl.ds(4 * t, 4)
        wide[rows, 0:1024] = q[t].astype(F32)
        for s in range(4):
            pair = kv[t, s].astype(F32)
            wide[pl.ds(4 * t + s, 1), 1024:1152] = pair[0:1]
            wide[pl.ds(4 * t + s, 1), 1152:1280] = pair[1:2]
        wide[rows, 1280:1408] = c[t].astype(F32)
    x0 = x[0].astype(F32)
    wide[pl.ds(0, 4), 1408:1792] = x0[:, 0:384]
    wide[pl.ds(4, 4), 1408:1536] = x0[:, 384:512]
    wide[pl.ds(4, 4), 1536:1664] = b[0].astype(F32)
    wide[pl.ds(4, 4), 1664:1672] = dt[0].astype(F32)
    item[...] = wide[...].astype(BF16)


def first_rows(shape):
    return lax.broadcasted_iota(jnp.int32, shape, 0) < 4


def sort_out_body(parents, inverse, *refs):
    rows, outs, held = refs[:4], refs[4:12], refs[12]
    me = lax.axis_index("replica")
    for k in range(4):
        held[k] = rows[k][...]
    first = first_rows((8, STEP_LANES))
    for k in range(8):
        dest = (me & 24) | ((me + k) & 7)
        pick = lambda source: ((me >> 3) - (source >> 3)) & 3
        for_child = held[pick(inverse[0, dest])].astype(F32)
        for_second = held[pick(inverse[1, dest])].astype(F32)
        carry = held[pick(source_of(parents, 1, dest))]
        outs[k][:, 0:STEP_LANES] = jnp.where(
            first, for_child[:, 0:STEP_LANES], for_second[:, 0:STEP_LANES]
        ).astype(BF16)
        outs[k][:, STEP_LANES:] = carry[:, STEP_LANES:]


def sort_back_body(parents, *refs):
    rows, outs, held = refs[:4], refs[4:12], refs[12]
    me = lax.axis_index("replica")
    for k in range(4):
        held[k] = rows[k][...]
    first = first_rows((8, BACK_LANES))
    for k in range(8):
        dest = (me & 24) | ((me + k) & 7)
        pick = lambda source: ((me >> 3) - (source >> 3)) & 3
        one = held[pick(source_of(parents, 0, dest))].astype(F32)
        two = held[pick(root_of(parents, dest))].astype(F32)
        outs[k][...] = jnp.where(first, one, two).astype(BF16)


def by_row(values, shape):
    row = lax.broadcasted_iota(jnp.int32, shape, 0)
    out = jnp.full(shape, values[-1], jnp.int32)
    for i in range(len(values) - 1):
        out = jnp.where(row == i, values[i], out)
    return out


def nt_dot(a, b):
    return lax.dot_general(a, b, (((1,), (1,)), ((), ())), preferred_element_type=F32)


def attend_body(parents, inverse, lengths, *refs):
    blocks = refs[:8]
    keys, values, state = refs[8:11]
    back, carry = refs[11:13]
    held = refs[13]
    me = lax.axis_index("replica")
    child = inverse[0, me]
    second = inverse[1, me]
    for k in range(8):
        held[k] = blocks[k][...]
    one = held[(me - child) & 7].astype(F32)
    two = held[(me - second) & 7].astype(F32)
    carry[...] = held[(me - source_of(parents, 1, me)) & 7][:, STEP_LANES:]
    item = jnp.where(
        first_rows((8, STEP_LANES)), one[:, 0:STEP_LANES], two[:, 0:STEP_LANES]
    )
    query = jnp.concatenate([item[:, h * HD : (h + 1) * HD] for h in range(8)], axis=0).astype(BF16)
    pads = jnp.zeros((120, HD), F32)
    new_keys = jnp.concatenate([item[:, 1024:1152], pads], axis=0).astype(BF16)
    new_values = jnp.concatenate([item[:, 1152:1280], pads], axis=0).astype(BF16)
    c_rows = item[:, 1280:1408].astype(BF16)
    ways = [parents[1, second * 4 + s] & 3 for s in range(4)]
    roots = [parents[0, child * 4 + s] & 3 for s in range(4)]
    roots += [parents[0, child * 4 + ways[s]] & 3 for s in range(4)]
    scale = HD ** (-0.5)

    root_rows = by_row(roots, (8, 1024))
    live = lax.broadcasted_iota(jnp.int32, (8, 1024), 1) < lengths[me]
    scores = jnp.zeros((8, 8, 1024), F32)
    for r in range(4):
        part = nt_dot(query, keys[r]).reshape(8, 8, 1024)
        scores = jnp.where((root_rows == r)[None], part, scores)
    scores = jnp.where(live[None], scores * scale, MASKED)

    row = lax.broadcasted_iota(jnp.int32, (8, HD), 0)
    column = lax.broadcasted_iota(jnp.int32, (8, HD), 1)
    way_rows = by_row([0, 1, 2, 3] + ways, (8, HD))
    seen = (column == row) | (column == way_rows)
    new_scores = nt_dot(query, new_keys).reshape(8, 8, HD) * scale
    new_scores = jnp.where(seen[None], new_scores, MASKED)

    top = jnp.maximum(
        jnp.max(scores, axis=-1, keepdims=True), jnp.max(new_scores, axis=-1, keepdims=True)
    )
    weights = jnp.exp(scores - top)
    new_weights = jnp.exp(new_scores - top)
    total = jnp.sum(weights, axis=-1, keepdims=True) + jnp.sum(new_weights, axis=-1, keepdims=True)
    mixed = jnp.dot(
        new_weights.reshape(64, HD).astype(BF16), new_values, preferred_element_type=F32
    )
    for r in range(4):
        mine = jnp.where((root_rows == r)[None], weights, 0.0).reshape(64, 1024).astype(BF16)
        mixed = mixed + jnp.dot(mine, values[r], preferred_element_type=F32)
    mixed = mixed / total.reshape(64, 1)
    for h in range(8):
        back[:, h * HD : (h + 1) * HD] = mixed[h * 8 : (h + 1) * 8].astype(BF16)

    root_wide = by_row(roots, (8, 512))
    read = jnp.zeros((8, 512), F32)
    for r in range(4):
        part = jnp.dot(c_rows, state[r], preferred_element_type=F32)
        read = jnp.where(root_wide == r, part, read)
    back[:, 1024:1536] = read.astype(BF16)


def per_head(ref, rows=8):
    head = lax.broadcasted_iota(jnp.int32, (rows, 512), 1) >> 6
    out = jnp.full((rows, 512), ref[7], F32)
    for h in range(7):
        out = jnp.where(head == h, ref[h], out)
    return out


def spread_heads(dt):
    head = lax.broadcasted_iota(jnp.int32, (HD, 512), 0)
    lane = lax.broadcasted_iota(jnp.int32, (HD, 512), 1) >> 6
    expand = (head == lane).astype(F32).astype(BF16)
    return jnp.dot(dt.astype(BF16), expand, preferred_element_type=F32)


def step_terms(dt, x, rate, bias):
    raw = spread_heads(dt) + bias
    step = jnp.maximum(raw, 0.0) + jnp.log1p(jnp.exp(-jnp.abs(raw)))
    return jnp.exp(-rate * step), step * x


def parent_rows(parents, me, carry, wide):
    folded = carry[...].astype(F32)
    wide[pl.ds(8, 4), 0:384] = folded[0:4]
    wide[pl.ds(8, 4), 384:768] = folded[4:8]
    wide[pl.ds(0, 4), :] = jnp.zeros((4, 768), F32)
    for s in range(4):
        way = parents[1, me * 4 + s] & 3
        wide[pl.ds(4 + s, 1), :] = wide[pl.ds(8 + way, 1), :]
    return wide[pl.ds(0, 8), :]


def stacked(ref, wide, lanes):
    wide[pl.ds(0, 4), 0:lanes] = ref[0].astype(F32)
    wide[pl.ds(4, 4), 0:lanes] = ref[1].astype(F32)
    return wide[pl.ds(0, 8), 0:lanes]


def mamba_body(parents, a_rate, dt_bias, skip, *refs):
    blocks = refs[:8]
    carry, x_in, z_in, dt_in, b_in, c_in, gain, proj = refs[8:16]
    attn, keep, send = refs[16:19]
    held, wide = refs[19:21]
    me = lax.axis_index("replica")
    core = lax.axis_index("tensor") & 1
    for k in range(8):
        held[k] = blocks[k][...]
    one = held[(me - source_of(parents, 0, me)) & 7].astype(F32)
    two = held[(me - root_of(parents, me)) & 7].astype(F32)
    attn[0] = one[0:4, 0:1024].astype(BF16)
    attn[1] = two[4:8, 0:1024].astype(BF16)
    first = first_rows((8, 512))
    read = jnp.where(first, one[:, 1024:1536], two[:, 1024:1536])

    rate = per_head(a_rate)
    bias = per_head(dt_bias)
    earlier = parent_rows(parents, me, carry, wide)
    decay_p, drive_p = step_terms(earlier[:, 640:768], earlier[:, 0:512], rate, bias)
    b_p = earlier[:, 512:640]
    wide[pl.ds(0, 8), 0:HD] = jnp.zeros((8, HD), F32)
    stacked(dt_in, wide, 8)
    dt = wide[pl.ds(0, 8), 0:HD]
    x = stacked(x_in, wide, 512)
    z = stacked(z_in, wide, 512)
    b = stacked(b_in, wide, HD)
    c = stacked(c_in, wide, HD)
    decay, drive = step_terms(dt, x, rate, bias)
    inner = decay_p * read + drive_p * jnp.sum(b_p * c, axis=-1, keepdims=True)
    inner = jnp.where(first, read, inner)
    out = decay * inner + drive * jnp.sum(b * c, axis=-1, keepdims=True) + per_head(skip) * x
    gated = out * (z / (1.0 + jnp.exp(-z)))
    mean = jnp.mean(gated * gated, axis=-1, keepdims=True)
    normed = (gated * lax.rsqrt(mean + 1e-05) * gain[...]).astype(BF16)
    for y in range(4):
        own = pl.multiple_of((2 * y + core) * 512, 512)
        other = pl.multiple_of((2 * y + 1 - core) * 512, 512)
        send[y] = jnp.dot(normed, proj[:, pl.ds(other, 512)], preferred_element_type=F32).astype(BF16)
        keep[y] = jnp.dot(normed, proj[:, pl.ds(own, 512)], preferred_element_type=F32).astype(BF16)


def core_sum_body(keep, came, *refs):
    outs, total = refs[:4], refs[4]
    y = lax.axis_index("tensor") >> 1
    total[...] = keep[...].astype(F32) + came[...].astype(F32)
    for k in range(4):
        outs[k][...] = total[(y + k) & 3].astype(BF16)


def last_sum_body(a, b, c, d, out):
    total = (a[...].astype(F32) + b[...].astype(F32)) + (c[...].astype(F32) + d[...].astype(F32))
    out[0] = total[0:4].astype(BF16)
    out[1] = total[4:8].astype(BF16)


def regroup_body(parents, came, out):
    for prompt in range(32):
        out[prompt] = came[root_of(parents, prompt)]


def advance_body(parents, a_rate, dt_bias, state, carry, x_in, dt_in, b_in, out, wide):
    me = lax.axis_index("replica")
    rate = per_head(a_rate)
    bias = per_head(dt_bias)
    earlier = parent_rows(parents, me, carry, wide)
    decay_p, drive_p = step_terms(earlier[:, 640:768], earlier[:, 0:512], rate, bias)
    b_p = earlier[:, 512:640]
    wide[pl.ds(0, 8), 0:HD] = jnp.zeros((8, HD), F32)
    stacked(dt_in, wide, 8)
    dt = wide[pl.ds(0, 8), 0:HD]
    x = stacked(x_in, wide, 512)
    b = stacked(b_in, wide, HD)
    decay, drive = step_terms(dt, x, rate, bias)
    columns_p = jnp.transpose(b_p)
    columns = jnp.transpose(b)
    source = source_of(parents, 1, me)
    for s in range(4):
        root = parents[0, source * 4 + (parents[1, me * 4 + s] & 3)] & 3
        r = 4 + s
        for i in range(8):
            rows = slice(i * 16, (i + 1) * 16)
            old = state[root * 8 + i].astype(F32)
            mid = decay_p[r : r + 1] * old + drive_p[r : r + 1] * columns_p[rows, r : r + 1]
            mid = mid.astype(BF16).astype(F32)
            new = decay[r : r + 1] * mid + drive[r : r + 1] * columns[rows, r : r + 1]
            out[s * 8 + i] = new.astype(BF16)


def along_x(array, k):
    return lax.ppermute(array, "replica", [(r, ((r + 8 * k) & 31)) for r in range(32)])


def along_z(array, k):
    return lax.ppermute(array, "replica", [(r, (r & 24) | ((r + k) & 7)) for r in range(32)])


def along_y(array, k):
    return lax.ppermute(array, "tensor", [(t, (t + 2 * k) & 7) for t in range(8)])


def across(array):
    return lax.ppermute(array, "tensor", [(t, t ^ 1) for t in range(8)])


def struct(shape, dtype=BF16):
    return jax.ShapeDtypeStruct(shape, dtype)


def per_device(
    ssm_state,
    kcache,
    vcache,
    lengths,
    parents,
    x_in,
    z_in,
    dt_in,
    b_in,
    c_in,
    q_in,
    kv_new,
    a_rate,
    dt_bias,
    skip,
    gain,
    out_proj,
):
    came = lax.all_to_all(ssm_state.reshape(32, 16, 512), "replica", 0, 0, tiled=True)

    item, inverse = call(
        pack_body,
        "pack",
        (struct((8, ITEM_LANES)), struct((2, 32), jnp.int32)),
        [SMEM] + [VMEM] * 6,
        (VMEM, SMEM),
        [pltpu.VMEM((8, ITEM_LANES), F32)],
    )(parents, q_in, kv_new, c_in, x_in, b_in, dt_in)
    rows = [item] + [along_x(item, k) for k in range(1, 4)]
    blocks = call(
        sort_out_body,
        "sort_out",
        (struct((8, ITEM_LANES)),) * 8,
        [SMEM, SMEM] + [VMEM] * 4,
        (VMEM,) * 8,
        [pltpu.VMEM((4, 8, ITEM_LANES), BF16)],
    )(parents, inverse, *rows)
    blocks = [blocks[0]] + [along_z(blocks[k], k) for k in range(1, 8)]
    back, carry = call(
        attend_body,
        "attend",
        (struct((8, BACK_LANES)), struct((8, CARRY_LANES))),
        [SMEM] * 3 + [VMEM] * 11,
        (VMEM, VMEM),
        [pltpu.VMEM((8, 8, ITEM_LANES), BF16)],
        (140000000, 3000000),
    )(parents, inverse, lengths, *blocks, kcache, vcache, ssm_state)
    rows = [back] + [along_x(back, k) for k in range(1, 4)]
    blocks = call(
        sort_back_body,
        "sort_back",
        (struct((8, BACK_LANES)),) * 8,
        [SMEM] + [VMEM] * 4,
        (VMEM,) * 8,
        [pltpu.VMEM((4, 8, BACK_LANES), BF16)],
    )(parents, *rows)
    blocks = [blocks[0]] + [along_z(blocks[k], k) for k in range(1, 8)]
    attn_out, keep, send = call(
        mamba_body,
        "mamba",
        (struct((2, 4, 1024)), struct((4, 8, 512)), struct((4, 8, 512))),
        [SMEM] * 4 + [VMEM] * 16,
        (VMEM,) * 3,
        [pltpu.VMEM((8, 8, BACK_LANES), BF16), pltpu.VMEM((16, 768), F32)],
        (40000000, 5000000),
    )(
        parents, a_rate, dt_bias, skip, *blocks, carry, x_in, z_in, dt_in, b_in, c_in,
        gain.reshape(1, 512), out_proj,
    )
    parts = call(
        core_sum_body,
        "core_sum",
        (struct((8, 512)),) * 4,
        [VMEM, VMEM],
        (VMEM,) * 4,
        [pltpu.VMEM((4, 8, 512), F32)],
    )(keep, across(send))
    mamba_out = call(last_sum_body, "last_sum", struct((2, 4, 512)), [VMEM] * 4, VMEM)(
        parts[0], *[along_y(parts[k], k) for k in range(1, 4)]
    )

    regrouped = call(
        regroup_body, "regroup", struct((32, 16, 512)), [SMEM, VMEM], VMEM
    )(parents, came)
    arrived = lax.all_to_all(regrouped, "replica", 0, 0, tiled=True)
    final_state = call(
        advance_body,
        "advance",
        struct((32, 16, 512)),
        [SMEM] * 3 + [VMEM] * 5,
        VMEM,
        [pltpu.VMEM((16, 768), F32)],
        (4000000, 1000000),
    )(parents, a_rate, dt_bias, arrived, carry, x_in, dt_in, b_in)
    return (final_state.reshape(4, 128, 512), mamba_out, attn_out)


def solution(mesh):
    return jax.shard_map(
        per_device,
        mesh=mesh,
        in_specs=(
            P("replica", None, "tensor"),
            P("replica", None, "tensor"),
            P("replica", None, "tensor"),
            P(),
            P(),
            P(None, "replica", "tensor"),
            P(None, "replica", "tensor"),
            P(None, "replica", "tensor"),
            P(None, "replica", None),
            P(None, "replica", None),
            P(None, "replica", "tensor"),
            P(None, "replica", None, "tensor"),
            P("tensor"),
            P("tensor"),
            P("tensor"),
            P("tensor"),
            P("tensor", None),
        ),
        out_specs=(
            P("replica", None, "tensor"),
            P(None, "replica", "tensor"),
            P(None, "replica", "tensor"),
        ),
        check_vma=False,
    )
```

```python
import functools

import jax
import jax.numpy as jnp
from jax import lax
from jax.experimental import pallas as pl
from jax.experimental.pallas import tpu as pltpu
from jax.sharding import PartitionSpec as P

F32 = jnp.float32
BF16 = jnp.bfloat16
HD = 128
ITEM_LANES = 1408
RESULT_LANES = 1536
CARRY_LANES = 384
BACK_LANES = RESULT_LANES + CARRY_LANES
MASKED = -1e30
MIB = 1024 * 1024

SMEM = pl.BlockSpec(memory_space=pltpu.SMEM)
VMEM = pl.BlockSpec(memory_space=pltpu.VMEM)
HBM = pl.BlockSpec(memory_space=pltpu.HBM)


def call(body, name, out_shape, in_specs, out_specs, scratch=(), flops=1000000, limit=32):
    return pl.pallas_call(
        body,
        name=name,
        out_shape=out_shape,
        in_specs=in_specs,
        out_specs=out_specs,
        scratch_shapes=list(scratch),
        compiler_params=pltpu.CompilerParams(vmem_limit_bytes=int(limit * MIB)),
        cost_estimate=pl.CostEstimate(flops=flops, bytes_accessed=0, transcendentals=0),
    )


def source_of(parents, step, prompt):
    return parents[step, prompt * 4] >> 2


def root_of(parents, prompt):
    return source_of(parents, 0, source_of(parents, 1, prompt))


def fetch(pairs, sems):
    copies = [pltpu.make_async_copy(src, dst, sems.at[i]) for i, (src, dst) in enumerate(pairs)]
    for copy in copies:
        copy.start()
    return copies


def pack_body(*refs):
    sources, (item, carry), wide, sems = refs[:6], refs[6:8], refs[14], refs[15]
    q, kv, c, x, b, dt = refs[8:14]
    copies = fetch(list(zip(sources, refs[8:14])), sems)
    for copy in copies:
        copy.wait()
    for t in range(2):
        rows = pl.ds(4 * t, 4)
        wide[rows, 0:1024] = q[t].astype(F32)
        for s in range(4):
            pair = kv[t, s].astype(F32)
            wide[pl.ds(4 * t + s, 1), 1024:1152] = pair[0:1]
            wide[pl.ds(4 * t + s, 1), 1152:1280] = pair[1:2]
        wide[rows, 1280:1408] = c[t].astype(F32)
    item[...] = wide[...].astype(BF16)
    wide[:, 0:CARRY_LANES] = jnp.zeros((8, CARRY_LANES), F32)
    x0 = x[0].astype(F32)
    wide[pl.ds(0, 4), 0:384] = x0[:, 0:384]
    wide[pl.ds(4, 4), 0:128] = x0[:, 384:512]
    wide[pl.ds(4, 4), 128:256] = b[0].astype(F32)
    wide[pl.ds(4, 4), 256:264] = dt[0].astype(F32)
    carry[...] = wide[:, 0:CARRY_LANES].astype(BF16)


def table_body(parents, lengths, table):
    for slot in range(128):
        table[0, slot] = parents[0, slot]
        table[1, slot] = parents[1, slot]
    for prompt in range(32):
        table[2, source_of(parents, 0, prompt)] = prompt
        table[3, root_of(parents, prompt)] = prompt
        table[4, prompt] = lengths[prompt]


def first_rows(shape):
    return lax.broadcasted_iota(jnp.int32, shape, 0) < 4


def bundle_body(own, up, down, out):
    out[0] = own[...]
    out[1] = up[...]
    out[2] = down[...]


def hold(held, own, up, down):
    for d, (ref, i) in enumerate(
        ((own, 0), (up, 0), (down, 1), (own, 1), (up, 1), (own, 2), (up, 2), (down, 0))
    ):
        held[d] = ref[i]


def stage_body(*refs):
    half = (len(refs) - 1) // 2
    for copy in fetch(list(zip(refs[:half], refs[half : 2 * half])), refs[-1]):
        copy.wait()


def sort_out_body(table, own, up, down, *refs):
    outs, held = refs[:4], refs[4]
    me = lax.axis_index("replica")
    hold(held, own, up, down)
    first = first_rows((8, ITEM_LANES))
    for k in range(4):
        dest = (me + 8 * k) & 31
        for_child = held[(me - table[2, dest]) & 7].astype(F32)
        for_second = held[(me - table[3, dest]) & 7].astype(F32)
        outs[k][...] = jnp.where(first, for_child, for_second).astype(BF16)


def bundle_back_body(own, one, two, three, out):
    for k, ref in enumerate((own, one, two, three)):
        out[k] = ref[...]


def sort_back_body(parents, own, up, down, *refs):
    outs, held = refs[:3], refs[3]
    me = lax.axis_index("replica")
    held[0], held[1], held[2] = own[...], up[...], down[...]
    first = first_rows((8, RESULT_LANES))
    for k, step in enumerate((0, 3, 5)):
        dest = (me & 24) | ((me + step) & 7)

        def pick(source):
            away = (me - source) & 7
            ring = jnp.where(away == 1, 1, jnp.where(away == 7, 2, 0))
            return held[ring, column(me, source)].astype(F32)

        one = pick(source_of(parents, 0, dest))[:, 0:RESULT_LANES]
        two = pick(root_of(parents, dest))[:, 0:RESULT_LANES]
        outs[k][:, 0:RESULT_LANES] = jnp.where(first, one, two).astype(BF16)
        outs[k][:, RESULT_LANES:] = pick(source_of(parents, 1, dest))[:, RESULT_LANES:].astype(BF16)


def came_by(me, source):
    away = (me - source) & 7
    up = (away >= 2) & (away <= 4)
    down = (away == 5) | (away == 6)
    return jnp.where(up, 1, jnp.where(down, 2, 0))


def column(me, source):
    return ((me >> 3) - (source >> 3)) & 3


def by_row(values, shape):
    row = lax.broadcasted_iota(jnp.int32, shape, 0)
    out = jnp.full(shape, values[-1], jnp.int32)
    for i in range(len(values) - 1):
        out = jnp.where(row == i, values[i], out)
    return out


def nt_dot(a, b):
    return lax.dot_general(a, b, (((1,), (1,)), ((), ())), preferred_element_type=F32)


def attend_body(parents, *refs):
    blocks = refs[:4]
    carry, keys, values, state, back, held = refs[4:10]
    me = lax.axis_index("replica")
    child = parents[2, me]
    second = parents[3, me]
    for k in range(4):
        held[k] = blocks[k][...]
    one = held[column(me, child)].astype(F32)
    two = held[column(me, second)].astype(F32)
    item = jnp.where(first_rows((8, ITEM_LANES)), one, two)
    back[:, RESULT_LANES:] = carry[...]

    query = jnp.concatenate([item[:, h * HD : (h + 1) * HD] for h in range(8)], axis=0).astype(BF16)
    pads = jnp.zeros((120, HD), F32)
    new_keys = jnp.concatenate([item[:, 1024:1152], pads], axis=0).astype(BF16)
    new_values = jnp.concatenate([item[:, 1152:1280], pads], axis=0).astype(BF16)
    c_rows = item[:, 1280:1408].astype(BF16)
    ways = [parents[1, second * 4 + s] & 3 for s in range(4)]
    roots = [parents[0, child * 4 + s] & 3 for s in range(4)]
    roots += [parents[0, child * 4 + ways[s]] & 3 for s in range(4)]
    scale = HD ** (-0.5)

    root_rows = by_row(roots, (8, 1024))
    live = lax.broadcasted_iota(jnp.int32, (8, 1024), 1) < parents[4, me]
    scores = jnp.zeros((8, 8, 1024), F32)
    for r in range(4):
        part = nt_dot(query, keys[r]).reshape(8, 8, 1024)
        scores = jnp.where((root_rows == r)[None], part, scores)
    scores = jnp.where(live[None], scores * scale, MASKED)

    row = lax.broadcasted_iota(jnp.int32, (8, HD), 0)
    key_at = lax.broadcasted_iota(jnp.int32, (8, HD), 1)
    way_rows = by_row([0, 1, 2, 3] + ways, (8, HD))
    seen = (key_at == row) | (key_at == way_rows)
    new_scores = nt_dot(query, new_keys).reshape(8, 8, HD) * scale
    new_scores = jnp.where(seen[None], new_scores, MASKED)

    top = jnp.maximum(
        jnp.max(scores, axis=-1, keepdims=True), jnp.max(new_scores, axis=-1, keepdims=True)
    )
    weights = jnp.exp(scores - top)
    new_weights = jnp.exp(new_scores - top)
    total = jnp.sum(weights, axis=-1, keepdims=True) + jnp.sum(new_weights, axis=-1, keepdims=True)
    mixed = jnp.dot(
        new_weights.reshape(64, HD).astype(BF16), new_values, preferred_element_type=F32
    )
    for r in range(4):
        mine = jnp.where((root_rows == r)[None], weights, 0.0).reshape(64, 1024).astype(BF16)
        mixed = mixed + jnp.dot(mine, values[r], preferred_element_type=F32)
    mixed = mixed / total.reshape(64, 1)
    for h in range(8):
        back[:, h * HD : (h + 1) * HD] = mixed[h * 8 : (h + 1) * 8].astype(BF16)

    root_wide = by_row(roots, (8, 512))
    read = jnp.zeros((8, 512), F32)
    for r in range(4):
        part = jnp.dot(c_rows, state[r], preferred_element_type=F32)
        read = jnp.where(root_wide == r, part, read)
    back[:, 1024:1536] = read.astype(BF16)


def per_head(ref, rows=8):
    head = lax.broadcasted_iota(jnp.int32, (rows, 512), 1) >> 6
    out = jnp.full((rows, 512), ref[7], F32)
    for h in range(7):
        out = jnp.where(head == h, ref[h], out)
    return out


def spread_heads(dt):
    head = lax.broadcasted_iota(jnp.int32, (HD, 512), 0)
    lane = lax.broadcasted_iota(jnp.int32, (HD, 512), 1) >> 6
    expand = (head == lane).astype(F32).astype(BF16)
    return jnp.dot(dt.astype(BF16), expand, preferred_element_type=F32)


def step_terms(dt, x, rate, bias):
    raw = spread_heads(dt) + bias
    step = jnp.maximum(raw, 0.0) + jnp.log1p(jnp.exp(-jnp.abs(raw)))
    return jnp.exp(-rate * step), step * x


def parent_rows(parents, me, carry, wide):
    folded = carry.astype(F32)
    wide[pl.ds(8, 4), 0:384] = folded[0:4]
    wide[pl.ds(8, 4), 384:768] = folded[4:8]
    wide[pl.ds(0, 4), :] = jnp.zeros((4, 768), F32)
    for s in range(4):
        way = parents[1, me * 4 + s] & 3
        wide[pl.ds(4 + s, 1), :] = wide[pl.ds(8 + way, 1), :]
    return wide[pl.ds(0, 8), :]


def stacked(ref, wide, lanes):
    wide[pl.ds(0, 4), 0:lanes] = ref[0].astype(F32)
    wide[pl.ds(4, 4), 0:lanes] = ref[1].astype(F32)
    return wide[pl.ds(0, 8), 0:lanes]


def mamba_body(parents, a_rate, dt_bias, skip, *refs):
    blocks = refs[:3]
    x_in, z_in, dt_in, b_in, c_in, gain, proj = refs[3:10]
    attn, keep, send, carry, held, wide = refs[10:16]
    me = lax.axis_index("replica")
    core = lax.axis_index("tensor") & 1
    for k in range(3):
        held[k] = blocks[k][...]
    one = held[came_by(me, source_of(parents, 0, me))].astype(F32)
    two = held[came_by(me, root_of(parents, me))].astype(F32)
    mine = held[came_by(me, source_of(parents, 1, me))][:, RESULT_LANES:]
    carry[...] = mine
    attn[0] = one[0:4, 0:1024].astype(BF16)
    attn[1] = two[4:8, 0:1024].astype(BF16)
    first = first_rows((8, 512))
    read = jnp.where(first, one[:, 1024:RESULT_LANES], two[:, 1024:RESULT_LANES])

    rate = per_head(a_rate)
    bias = per_head(dt_bias)
    earlier = parent_rows(parents, me, mine, wide)
    decay_p, drive_p = step_terms(earlier[:, 640:768], earlier[:, 0:512], rate, bias)
    b_p = earlier[:, 512:640]
    wide[pl.ds(0, 8), 0:HD] = jnp.zeros((8, HD), F32)
    stacked(dt_in, wide, 8)
    dt = wide[pl.ds(0, 8), 0:HD]
    x = stacked(x_in, wide, 512)
    z = stacked(z_in, wide, 512)
    b = stacked(b_in, wide, HD)
    c = stacked(c_in, wide, HD)
    decay, drive = step_terms(dt, x, rate, bias)
    inner = decay_p * read + drive_p * jnp.sum(b_p * c, axis=-1, keepdims=True)
    inner = jnp.where(first, read, inner)
    out = decay * inner + drive * jnp.sum(b * c, axis=-1, keepdims=True) + per_head(skip) * x
    gated = out * (z / (1.0 + jnp.exp(-z)))
    mean = jnp.mean(gated * gated, axis=-1, keepdims=True)
    normed = (gated * lax.rsqrt(mean + 1e-05) * gain[...]).astype(BF16)
    for y in range(4):
        for target, parity in ((send, 1 - core), (keep, core)):
            span = pl.ds(pl.multiple_of((2 * y + parity) * 512, 512), 512)
            part = jnp.dot(normed, proj[:, span], preferred_element_type=F32)
            target[y] = part.astype(BF16)


def core_sum_body(keep, came, *refs):
    outs, total = refs[:4], refs[4]
    y = lax.axis_index("tensor") >> 1
    total[...] = keep[...].astype(F32) + came[...].astype(F32)
    for k in range(4):
        outs[k][...] = total[(y + k) & 3].astype(BF16)


def last_sum_body(a, b, c, d, out):
    total = (a[...].astype(F32) + b[...].astype(F32)) + (c[...].astype(F32) + d[...].astype(F32))
    out[0] = total[0:4].astype(BF16)
    out[1] = total[4:8].astype(BF16)


def regroup_body(parents, came, _, out):
    for prompt in range(32):
        out[prompt] = came[root_of(parents, prompt)]


def advance_body(parents, a_rate, dt_bias, state, carry, x_in, dt_in, b_in, out, wide):
    me = lax.axis_index("replica")
    rate = per_head(a_rate)
    bias = per_head(dt_bias)
    earlier = parent_rows(parents, me, carry[...], wide)
    decay_p, drive_p = step_terms(earlier[:, 640:768], earlier[:, 0:512], rate, bias)
    b_p = earlier[:, 512:640]
    wide[pl.ds(0, 8), 0:HD] = jnp.zeros((8, HD), F32)
    stacked(dt_in, wide, 8)
    dt = wide[pl.ds(0, 8), 0:HD]
    x = stacked(x_in, wide, 512)
    b = stacked(b_in, wide, HD)
    decay, drive = step_terms(dt, x, rate, bias)
    columns_p = jnp.transpose(b_p)
    columns = jnp.transpose(b)
    source = source_of(parents, 1, me)
    for s in range(4):
        root = parents[0, source * 4 + (parents[1, me * 4 + s] & 3)] & 3
        r = 4 + s
        for i in range(8):
            rows = slice(i * 16, (i + 1) * 16)
            old = state[root * 8 + i].astype(F32)
            mid = decay_p[r : r + 1] * old + drive_p[r : r + 1] * columns_p[rows, r : r + 1]
            mid = mid.astype(BF16).astype(F32)
            new = decay[r : r + 1] * mid + drive[r : r + 1] * columns[rows, r : r + 1]
            out[s * 8 + i] = new.astype(BF16)


def along_x(array, k):
    return lax.ppermute(array, "replica", [(r, ((r + 8 * k) & 31)) for r in range(32)])


def along_z(array, k):
    return lax.ppermute(array, "replica", [(r, (r & 24) | ((r + k) & 7)) for r in range(32)])


def along_y(array, k):
    return lax.ppermute(array, "tensor", [(t, (t + 2 * k) & 7) for t in range(8)])


def across(array):
    return lax.ppermute(array, "tensor", [(t, t ^ 1) for t in range(8)])


def struct(shape, dtype=BF16):
    return jax.ShapeDtypeStruct(shape, dtype)


def per_device(
    ssm_state,
    kcache,
    vcache,
    lengths,
    parents,
    x_in,
    z_in,
    dt_in,
    b_in,
    c_in,
    q_in,
    kv_new,
    a_rate,
    dt_bias,
    skip,
    gain,
    out_proj,
):
    item, carry = call(
        pack_body,
        "pack",
        (struct((8, ITEM_LANES)), struct((8, CARRY_LANES))),
        [HBM] * 6,
        (VMEM,) * 2,
        [
            pltpu.VMEM((2, 4, 1024), BF16),
            pltpu.VMEM((2, 4, 2, 128), BF16),
            pltpu.VMEM((2, 4, 128), BF16),
            pltpu.VMEM((2, 4, 512), BF16),
            pltpu.VMEM((2, 4, 128), BF16),
            pltpu.VMEM((2, 4, 8), BF16),
            pltpu.VMEM((8, ITEM_LANES), F32),
            pltpu.SemaphoreType.DMA((6,)),
        ],
        limit=60,
    )(q_in, kv_new, c_in, x_in, b_in, dt_in)
    item, parents = lax.optimization_barrier((item, parents))
    table = call(table_body, "table", struct((8, 128), jnp.int32), [SMEM] * 2, SMEM)(
        parents, lengths
    )
    came_up, came_down = along_z(item, 3), along_z(item, 5)
    item, table, *staged = lax.optimization_barrier((item, table, kcache, vcache, ssm_state))
    bundle = call(
        bundle_body, "bundle", struct((3, 8, ITEM_LANES)), [VMEM] * 3, VMEM
    )(item, came_up, came_down)
    up, down = along_z(bundle, 1), along_z(bundle, 7)
    keys, values, state = call(
        stage_body,
        "stage",
        (struct((4, 1024, 128)), struct((4, 1024, 128)), struct((4, 128, 512))),
        [HBM] * 3,
        (VMEM,) * 3,
        [pltpu.SemaphoreType.DMA((3,))],
    )(*staged)
    bundle, keys, values, state = lax.optimization_barrier((bundle, keys, values, state))
    blocks = call(
        sort_out_body,
        "sort_out",
        (struct((8, ITEM_LANES)),) * 4,
        [SMEM] + [VMEM] * 3,
        (VMEM,) * 4,
        [pltpu.VMEM((8, 8, ITEM_LANES), BF16)],
    )(table, bundle, up, down)
    own_block, moving = lax.optimization_barrier((blocks[0], ssm_state))
    blocks = [own_block] + list(blocks[1:])
    came = lax.all_to_all(moving.reshape(32, 16, 512), "replica", 0, 0, tiled=True)
    blocks = [blocks[0]] + [along_x(blocks[k], k) for k in range(1, 4)]
    back = call(
        attend_body,
        "attend",
        struct((8, BACK_LANES)),
        [SMEM] + [VMEM] * 8,
        VMEM,
        [pltpu.VMEM((4, 8, ITEM_LANES), BF16)],
        flops=50000000000,
    )(table, *blocks, carry, keys, values, state)
    rows = call(
        bundle_back_body, "bundle_back", struct((4, 8, BACK_LANES)), [VMEM] * 4, VMEM
    )(back, *[along_x(back, k) for k in range(1, 4)])
    up, down = along_z(rows, 1), along_z(rows, 7)
    blocks = call(
        sort_back_body,
        "sort_back",
        (struct((8, BACK_LANES)),) * 3,
        [SMEM] + [VMEM] * 3,
        (VMEM,) * 3,
        [pltpu.VMEM((3, 4, 8, BACK_LANES), BF16)],
    )(table, rows, up, down)
    regrouped = call(
        regroup_body, "regroup", struct((32, 16, 512)), [SMEM, VMEM, HBM], VMEM
    )(table, came, rows)
    own_block, regrouped, weights = lax.optimization_barrier((blocks[0], regrouped, out_proj))
    weights = call(
        stage_body,
        "stage_proj",
        struct((512, 4096)),
        [HBM],
        VMEM,
        [pltpu.SemaphoreType.DMA((1,))],
    )(weights)
    arrived = lax.all_to_all(regrouped, "replica", 0, 0, tiled=True)
    blocks = [own_block, along_z(blocks[1], 3), along_z(blocks[2], 5)]
    attn_out, keep, send, carry = call(
        mamba_body,
        "mamba",
        (
            struct((2, 4, 1024)),
            struct((4, 8, 512)),
            struct((4, 8, 512)),
            struct((8, CARRY_LANES)),
        ),
        [SMEM] * 4 + [VMEM] * 10,
        (VMEM,) * 4,
        [
            pltpu.VMEM((3, 8, BACK_LANES), BF16),
            pltpu.VMEM((16, 768), F32),
        ],
        flops=50000000000,
    )(
        table, a_rate, dt_bias, skip, *blocks, x_in, z_in, dt_in, b_in, c_in,
        gain.reshape(1, 512), weights,
    )
    parts = call(
        core_sum_body,
        "core_sum",
        (struct((8, 512)),) * 4,
        [VMEM, VMEM],
        (VMEM,) * 4,
        [pltpu.VMEM((4, 8, 512), F32)],
    )(keep, across(send))
    final_state = call(
        advance_body,
        "advance",
        struct((32, 16, 512)),
        [SMEM] * 3 + [VMEM] * 5,
        VMEM,
        [pltpu.VMEM((16, 768), F32)],
    )(table, a_rate, dt_bias, arrived, carry, x_in, dt_in, b_in)
    own_part, final_state = lax.optimization_barrier((parts[0], final_state))
    mamba_out = call(last_sum_body, "last_sum", struct((2, 4, 512)), [VMEM] * 4, VMEM)(
        own_part, *[along_y(parts[k], k) for k in range(1, 4)]
    )
    return (final_state.reshape(4, 128, 512), mamba_out, attn_out)


def solution(mesh):
    return jax.shard_map(
        per_device,
        mesh=mesh,
        in_specs=(
            P("replica", None, "tensor"),
            P("replica", None, "tensor"),
            P("replica", None, "tensor"),
            P(),
            P(),
            P(None, "replica", "tensor"),
            P(None, "replica", "tensor"),
            P(None, "replica", "tensor"),
            P(None, "replica", None),
            P(None, "replica", None),
            P(None, "replica", "tensor"),
            P(None, "replica", None, "tensor"),
            P("tensor"),
            P("tensor"),
            P("tensor"),
            P("tensor"),
            P("tensor", None),
        ),
        out_specs=(
            P("replica", None, "tensor"),
            P(None, "replica", "tensor"),
            P(None, "replica", "tensor"),
        ),
        check_vma=False,
    )
```

```python
import functools

import jax
import jax.numpy as jnp
from jax import lax
from jax.experimental import pallas as pl
from jax.experimental.pallas import tpu as pltpu
from jax.sharding import PartitionSpec as P

F32 = jnp.float32
BF16 = jnp.bfloat16
HD = 128
STEP_LANES = 1408
CARRY_LANES = 384
ITEM_LANES = STEP_LANES + CARRY_LANES
BACK_LANES = 1536
MASKED = -1e30
MIB = 1024 * 1024

SMEM = pl.BlockSpec(memory_space=pltpu.SMEM)
VMEM = pl.BlockSpec(memory_space=pltpu.VMEM)
HBM = pl.BlockSpec(memory_space=pltpu.HBM)


def call(body, name, out_shape, in_specs, out_specs, scratch=(), flops=1000000, limit=16):
    return pl.pallas_call(
        body,
        name=name,
        out_shape=out_shape,
        in_specs=in_specs,
        out_specs=out_specs,
        scratch_shapes=list(scratch),
        compiler_params=pltpu.CompilerParams(vmem_limit_bytes=int(limit * MIB)),
        cost_estimate=pl.CostEstimate(flops=flops, bytes_accessed=0, transcendentals=0),
    )


def source_of(parents, step, prompt):
    return parents[step, prompt * 4] >> 2


def root_of(parents, prompt):
    return source_of(parents, 0, source_of(parents, 1, prompt))


def fetch(pairs, sems):
    copies = [pltpu.make_async_copy(src, dst, sems.at[i]) for i, (src, dst) in enumerate(pairs)]
    for copy in copies:
        copy.start()
    return copies


def pack_body(*refs):
    sources, item, wide, sems = refs[:6], refs[6], refs[13], refs[14]
    q, kv, c, x, b, dt = refs[7:13]
    copies = fetch(list(zip(sources, refs[7:13])), sems)
    wide[:, STEP_LANES:] = jnp.zeros((8, CARRY_LANES), F32)
    for copy in copies:
        copy.wait()
    for t in range(2):
        rows = pl.ds(4 * t, 4)
        wide[rows, 0:1024] = q[t].astype(F32)
        for s in range(4):
            pair = kv[t, s].astype(F32)
            wide[pl.ds(4 * t + s, 1), 1024:1152] = pair[0:1]
            wide[pl.ds(4 * t + s, 1), 1152:1280] = pair[1:2]
        wide[rows, 1280:1408] = c[t].astype(F32)
    x0 = x[0].astype(F32)
    wide[pl.ds(0, 4), 1408:1792] = x0[:, 0:384]
    wide[pl.ds(4, 4), 1408:1536] = x0[:, 384:512]
    wide[pl.ds(4, 4), 1536:1664] = b[0].astype(F32)
    wide[pl.ds(4, 4), 1664:1672] = dt[0].astype(F32)
    item[...] = wide[...].astype(BF16)


def table_body(parents, lengths, table):
    for slot in range(128):
        table[0, slot] = parents[0, slot]
        table[1, slot] = parents[1, slot]
    for prompt in range(32):
        table[2, source_of(parents, 0, prompt)] = prompt
        table[3, root_of(parents, prompt)] = prompt
        table[4, prompt] = lengths[prompt]


def first_rows(shape):
    return lax.broadcasted_iota(jnp.int32, shape, 0) < 4


def bundle_body(own, up, down, out):
    out[0] = own[...]
    out[1] = up[...]
    out[2] = down[...]


def hold(held, own, up, down):
    for d, (ref, i) in enumerate(
        ((own, 0), (up, 0), (down, 1), (own, 1), (up, 1), (own, 2), (up, 2), (down, 0))
    ):
        held[d] = ref[i]


def stage_quarters_body(source, *refs):
    outs, sems = refs[:4], refs[4]
    pairs = [(source.at[:, pl.ds(1024 * y, 1024)], outs[y]) for y in range(4)]
    for copy in fetch(pairs, sems):
        copy.wait()


def stage_body(*refs):
    half = (len(refs) - 1) // 2
    for copy in fetch(list(zip(refs[:half], refs[half : 2 * half])), refs[-1]):
        copy.wait()


def sort_out_body(table, own, up, down, *refs):
    outs, held = refs[:4], refs[4]
    me = lax.axis_index("replica")
    hold(held, own, up, down)
    first = first_rows((8, STEP_LANES))
    for k in range(4):
        dest = (me + 8 * k) & 31
        for_child = held[(me - table[2, dest]) & 7].astype(F32)
        for_second = held[(me - table[3, dest]) & 7].astype(F32)
        carry = held[(me - source_of(table, 1, dest)) & 7]
        outs[k][:, 0:STEP_LANES] = jnp.where(
            first, for_child[:, 0:STEP_LANES], for_second[:, 0:STEP_LANES]
        ).astype(BF16)
        outs[k][:, STEP_LANES:] = carry[:, STEP_LANES:]


def bundle_back_body(own, one, two, three, out):
    for k, ref in enumerate((own, one, two, three)):
        out[k] = ref[...]


def sort_back_body(parents, own, up, down, *refs):
    outs, held = refs[:3], refs[3]
    me = lax.axis_index("replica")
    held[0], held[1], held[2] = own[...], up[...], down[...]
    first = first_rows((8, BACK_LANES))
    for k, step in enumerate((0, 3, 5)):
        dest = (me & 24) | ((me + step) & 7)

        def pick(source):
            away = (me - source) & 7
            ring = jnp.where(away == 1, 1, jnp.where(away == 7, 2, 0))
            return held[ring, column(me, source)].astype(F32)

        one = pick(source_of(parents, 0, dest))
        two = pick(root_of(parents, dest))
        outs[k][...] = jnp.where(first, one, two).astype(BF16)


def came_by(me, source):
    away = (me - source) & 7
    up = (away >= 2) & (away <= 4)
    down = (away == 5) | (away == 6)
    return jnp.where(up, 1, jnp.where(down, 2, 0))


def column(me, source):
    return ((me >> 3) - (source >> 3)) & 3


def by_row(values, shape):
    row = lax.broadcasted_iota(jnp.int32, shape, 0)
    out = jnp.full(shape, values[-1], jnp.int32)
    for i in range(len(values) - 1):
        out = jnp.where(row == i, values[i], out)
    return out


def nt_dot(a, b):
    return lax.dot_general(a, b, (((1,), (1,)), ((), ())), preferred_element_type=F32)


def attend_body(parents, *refs):
    blocks = refs[:4]
    keys, values, state, back, carry, held = refs[4:10]
    me = lax.axis_index("replica")
    child = parents[2, me]
    second = parents[3, me]
    for k in range(4):
        held[k] = blocks[k][...]
    one = held[column(me, child)].astype(F32)
    two = held[column(me, second)].astype(F32)
    item = jnp.where(first_rows((8, STEP_LANES)), one[:, 0:STEP_LANES], two[:, 0:STEP_LANES])
    carry[...] = held[column(me, source_of(parents, 1, me))][:, STEP_LANES:]

    query = jnp.concatenate([item[:, h * HD : (h + 1) * HD] for h in range(8)], axis=0).astype(BF16)
    pads = jnp.zeros((120, HD), F32)
    new_keys = jnp.concatenate([item[:, 1024:1152], pads], axis=0).astype(BF16)
    new_values = jnp.concatenate([item[:, 1152:1280], pads], axis=0).astype(BF16)
    c_rows = item[:, 1280:1408].astype(BF16)
    ways = [parents[1, second * 4 + s] & 3 for s in range(4)]
    roots = [parents[0, child * 4 + s] & 3 for s in range(4)]
    roots += [parents[0, child * 4 + ways[s]] & 3 for s in range(4)]
    scale = HD ** (-0.5)

    root_rows = by_row(roots, (8, 1024))
    live = lax.broadcasted_iota(jnp.int32, (8, 1024), 1) < parents[4, me]
    scores = jnp.zeros((8, 8, 1024), F32)
    for r in range(4):
        part = nt_dot(query, keys[r]).reshape(8, 8, 1024)
        scores = jnp.where((root_rows == r)[None], part, scores)
    scores = jnp.where(live[None], scores * scale, MASKED)

    row = lax.broadcasted_iota(jnp.int32, (8, HD), 0)
    key_at = lax.broadcasted_iota(jnp.int32, (8, HD), 1)
    way_rows = by_row([0, 1, 2, 3] + ways, (8, HD))
    seen = (key_at == row) | (key_at == way_rows)
    new_scores = nt_dot(query, new_keys).reshape(8, 8, HD) * scale
    new_scores = jnp.where(seen[None], new_scores, MASKED)

    top = jnp.maximum(
        jnp.max(scores, axis=-1, keepdims=True), jnp.max(new_scores, axis=-1, keepdims=True)
    )
    weights = jnp.exp(scores - top)
    new_weights = jnp.exp(new_scores - top)
    total = jnp.sum(weights, axis=-1, keepdims=True) + jnp.sum(new_weights, axis=-1, keepdims=True)
    mixed = jnp.dot(
        new_weights.reshape(64, HD).astype(BF16), new_values, preferred_element_type=F32
    )
    for r in range(4):
        mine = jnp.where((root_rows == r)[None], weights, 0.0).reshape(64, 1024).astype(BF16)
        mixed = mixed + jnp.dot(mine, values[r], preferred_element_type=F32)
    mixed = mixed / total.reshape(64, 1)
    for h in range(8):
        back[:, h * HD : (h + 1) * HD] = mixed[h * 8 : (h + 1) * 8].astype(BF16)

    root_wide = by_row(roots, (8, 512))
    read = jnp.zeros((8, 512), F32)
    for r in range(4):
        part = jnp.dot(c_rows, state[r], preferred_element_type=F32)
        read = jnp.where(root_wide == r, part, read)
    back[:, 1024:1536] = read.astype(BF16)


def per_head(ref, rows=8):
    head = lax.broadcasted_iota(jnp.int32, (rows, 512), 1) >> 6
    out = jnp.full((rows, 512), ref[7], F32)
    for h in range(7):
        out = jnp.where(head == h, ref[h], out)
    return out


def spread_heads(dt):
    head = lax.broadcasted_iota(jnp.int32, (HD, 512), 0)
    lane = lax.broadcasted_iota(jnp.int32, (HD, 512), 1) >> 6
    expand = (head == lane).astype(F32).astype(BF16)
    return jnp.dot(dt.astype(BF16), expand, preferred_element_type=F32)


def step_terms(dt, x, rate, bias):
    raw = spread_heads(dt) + bias
    step = jnp.maximum(raw, 0.0) + jnp.log1p(jnp.exp(-jnp.abs(raw)))
    return jnp.exp(-rate * step), step * x


def parent_rows(parents, me, carry, wide):
    folded = carry.astype(F32)
    wide[pl.ds(8, 4), 0:384] = folded[0:4]
    wide[pl.ds(8, 4), 384:768] = folded[4:8]
    wide[pl.ds(0, 4), :] = jnp.zeros((4, 768), F32)
    for s in range(4):
        way = parents[1, me * 4 + s] & 3
        wide[pl.ds(4 + s, 1), :] = wide[pl.ds(8 + way, 1), :]
    return wide[pl.ds(0, 8), :]


def stacked(ref, wide, lanes):
    wide[pl.ds(0, 4), 0:lanes] = ref[0].astype(F32)
    wide[pl.ds(4, 4), 0:lanes] = ref[1].astype(F32)
    return wide[pl.ds(0, 8), 0:lanes]


def mamba_body(parents, a_rate, dt_bias, skip, *refs):
    blocks = refs[:3]
    carry, x_in, z_in, dt_in, b_in, c_in, gain = refs[3:10]
    proj = refs[10:14]
    attn, keep, send, held, wide = refs[14:19]
    me = lax.axis_index("replica")
    core = lax.axis_index("tensor") & 1
    for k in range(3):
        held[k] = blocks[k][...]
    one = held[came_by(me, source_of(parents, 0, me))].astype(F32)
    two = held[came_by(me, root_of(parents, me))].astype(F32)
    attn[0] = one[0:4, 0:1024].astype(BF16)
    attn[1] = two[4:8, 0:1024].astype(BF16)
    first = first_rows((8, 512))
    read = jnp.where(first, one[:, 1024:BACK_LANES], two[:, 1024:BACK_LANES])

    rate = per_head(a_rate)
    bias = per_head(dt_bias)
    earlier = parent_rows(parents, me, carry[...], wide)
    decay_p, drive_p = step_terms(earlier[:, 640:768], earlier[:, 0:512], rate, bias)
    b_p = earlier[:, 512:640]
    wide[pl.ds(0, 8), 0:HD] = jnp.zeros((8, HD), F32)
    stacked(dt_in, wide, 8)
    dt = wide[pl.ds(0, 8), 0:HD]
    x = stacked(x_in, wide, 512)
    z = stacked(z_in, wide, 512)
    b = stacked(b_in, wide, HD)
    c = stacked(c_in, wide, HD)
    decay, drive = step_terms(dt, x, rate, bias)
    inner = decay_p * read + drive_p * jnp.sum(b_p * c, axis=-1, keepdims=True)
    inner = jnp.where(first, read, inner)
    out = decay * inner + drive * jnp.sum(b * c, axis=-1, keepdims=True) + per_head(skip) * x
    gated = out * (z / (1.0 + jnp.exp(-z)))
    mean = jnp.mean(gated * gated, axis=-1, keepdims=True)
    normed = (gated * lax.rsqrt(mean + 1e-05) * gain[...]).astype(BF16)
    for y in range(4):
        for target, parity in ((send, 1 - core), (keep, core)):
            span = pl.ds(pl.multiple_of(parity * 512, 512), 512)
            part = jnp.dot(normed, proj[y][:, span], preferred_element_type=F32)
            target[y] = part.astype(BF16)


def core_sum_body(keep, came, *refs):
    outs, total = refs[:4], refs[4]
    y = lax.axis_index("tensor") >> 1
    total[...] = keep[...].astype(F32) + came[...].astype(F32)
    for k in range(4):
        outs[k][...] = total[(y + k) & 3].astype(BF16)


def last_sum_body(a, b, c, d, out):
    total = (a[...].astype(F32) + b[...].astype(F32)) + (c[...].astype(F32) + d[...].astype(F32))
    out[0] = total[0:4].astype(BF16)
    out[1] = total[4:8].astype(BF16)


def regroup_body(parents, came, _, out):
    for prompt in range(32):
        out[prompt] = came[root_of(parents, prompt)]


def advance_body(parents, a_rate, dt_bias, state, carry, x_in, dt_in, b_in, out, wide):
    me = lax.axis_index("replica")
    rate = per_head(a_rate)
    bias = per_head(dt_bias)
    earlier = parent_rows(parents, me, carry[...], wide)
    decay_p, drive_p = step_terms(earlier[:, 640:768], earlier[:, 0:512], rate, bias)
    b_p = earlier[:, 512:640]
    wide[pl.ds(0, 8), 0:HD] = jnp.zeros((8, HD), F32)
    stacked(dt_in, wide, 8)
    dt = wide[pl.ds(0, 8), 0:HD]
    x = stacked(x_in, wide, 512)
    b = stacked(b_in, wide, HD)
    decay, drive = step_terms(dt, x, rate, bias)
    columns_p = jnp.transpose(b_p)
    columns = jnp.transpose(b)
    source = source_of(parents, 1, me)
    for s in range(4):
        root = parents[0, source * 4 + (parents[1, me * 4 + s] & 3)] & 3
        r = 4 + s
        for i in range(8):
            rows = slice(i * 16, (i + 1) * 16)
            old = state[root * 8 + i].astype(F32)
            mid = decay_p[r : r + 1] * old + drive_p[r : r + 1] * columns_p[rows, r : r + 1]
            mid = mid.astype(BF16).astype(F32)
            new = decay[r : r + 1] * mid + drive[r : r + 1] * columns[rows, r : r + 1]
            out[s * 8 + i] = new.astype(BF16)


def along_x(array, k):
    return lax.ppermute(array, "replica", [(r, ((r + 8 * k) & 31)) for r in range(32)])


def along_z(array, k):
    return lax.ppermute(array, "replica", [(r, (r & 24) | ((r + k) & 7)) for r in range(32)])


def along_y(array, k):
    return lax.ppermute(array, "tensor", [(t, (t + 2 * k) & 7) for t in range(8)])


def across(array):
    return lax.ppermute(array, "tensor", [(t, t ^ 1) for t in range(8)])


def struct(shape, dtype=BF16):
    return jax.ShapeDtypeStruct(shape, dtype)


def per_device(
    ssm_state,
    kcache,
    vcache,
    lengths,
    parents,
    x_in,
    z_in,
    dt_in,
    b_in,
    c_in,
    q_in,
    kv_new,
    a_rate,
    dt_bias,
    skip,
    gain,
    out_proj,
):
    item = call(
        pack_body,
        "pack",
        struct((8, ITEM_LANES)),
        [HBM] * 6,
        VMEM,
        [
            pltpu.VMEM((2, 4, 1024), BF16),
            pltpu.VMEM((2, 4, 2, 128), BF16),
            pltpu.VMEM((2, 4, 128), BF16),
            pltpu.VMEM((2, 4, 512), BF16),
            pltpu.VMEM((2, 4, 128), BF16),
            pltpu.VMEM((2, 4, 8), BF16),
            pltpu.VMEM((8, ITEM_LANES), F32),
            pltpu.SemaphoreType.DMA((6,)),
        ],
        limit=60,
    )(q_in, kv_new, c_in, x_in, b_in, dt_in)
    item, parents = lax.optimization_barrier((item, parents))
    table = call(table_body, "table", struct((8, 128), jnp.int32), [SMEM] * 2, SMEM)(
        parents, lengths
    )
    came_up, came_down = along_z(item, 3), along_z(item, 5)
    item, table, *staged = lax.optimization_barrier((item, table, kcache, vcache, ssm_state))
    bundle = call(
        bundle_body, "bundle", struct((3, 8, ITEM_LANES)), [VMEM] * 3, VMEM
    )(item, came_up, came_down)
    up, down = along_z(bundle, 1), along_z(bundle, 7)
    keys, values, state = call(
        stage_body,
        "stage",
        (struct((4, 1024, 128)), struct((4, 1024, 128)), struct((4, 128, 512))),
        [HBM] * 3,
        (VMEM,) * 3,
        [pltpu.SemaphoreType.DMA((3,))],
    )(*staged)
    bundle, keys, values, state = lax.optimization_barrier((bundle, keys, values, state))
    blocks = call(
        sort_out_body,
        "sort_out",
        (struct((8, ITEM_LANES)),) * 4,
        [SMEM] + [VMEM] * 3,
        (VMEM,) * 4,
        [pltpu.VMEM((8, 8, ITEM_LANES), BF16)],
    )(table, bundle, up, down)
    own_block, moving = lax.optimization_barrier((blocks[0], ssm_state))
    blocks = [own_block] + list(blocks[1:])
    came = lax.all_to_all(moving.reshape(32, 16, 512), "replica", 0, 0, tiled=True)
    blocks = [blocks[0]] + [along_x(blocks[k], k) for k in range(1, 4)]
    back, carry = call(
        attend_body,
        "attend",
        (struct((8, BACK_LANES)), struct((8, CARRY_LANES))),
        [SMEM] + [VMEM] * 7,
        (VMEM,) * 2,
        [pltpu.VMEM((4, 8, ITEM_LANES), BF16)],
        flops=50000000000,
    )(table, *blocks, keys, values, state)
    back, weights = lax.optimization_barrier((back, out_proj))
    weights = call(
        stage_quarters_body,
        "stage_proj",
        (struct((512, 1024)),) * 4,
        [HBM],
        (VMEM,) * 4,
        [pltpu.SemaphoreType.DMA((4,))],
    )(weights)
    others = [along_x(back, k) for k in range(1, 4)]
    back, *weights = lax.optimization_barrier((back, *weights))
    rows = call(
        bundle_back_body, "bundle_back", struct((4, 8, BACK_LANES)), [VMEM] * 4, VMEM
    )(back, *others)
    up, down = along_z(rows, 1), along_z(rows, 7)
    regrouped = call(
        regroup_body, "regroup", struct((32, 16, 512)), [SMEM, VMEM, HBM], VMEM
    )(table, came, rows)
    rows, regrouped = lax.optimization_barrier((rows, regrouped))
    blocks = call(
        sort_back_body,
        "sort_back",
        (struct((8, BACK_LANES)),) * 3,
        [SMEM] + [VMEM] * 3,
        (VMEM,) * 3,
        [pltpu.VMEM((3, 4, 8, BACK_LANES), BF16)],
    )(table, rows, up, down)
    own_block, regrouped = lax.optimization_barrier((blocks[0], regrouped))
    arrived = lax.all_to_all(regrouped, "replica", 0, 0, tiled=True)
    blocks = [own_block, along_z(blocks[1], 3), along_z(blocks[2], 5)]
    attn_out, keep, send = call(
        mamba_body,
        "mamba",
        (
            struct((2, 4, 1024)),
            struct((4, 8, 512)),
            struct((4, 8, 512)),
        ),
        [SMEM] * 4 + [VMEM] * 14,
        (VMEM,) * 3,
        [
            pltpu.VMEM((3, 8, BACK_LANES), BF16),
            pltpu.VMEM((16, 768), F32),
        ],
        flops=50000000000,
    )(
        table, a_rate, dt_bias, skip, *blocks, carry, x_in, z_in, dt_in, b_in, c_in,
        gain.reshape(1, 512), *weights,
    )
    parts = call(
        core_sum_body,
        "core_sum",
        (struct((8, 512)),) * 4,
        [VMEM, VMEM],
        (VMEM,) * 4,
        [pltpu.VMEM((4, 8, 512), F32)],
    )(keep, across(send))
    final_state = call(
        advance_body,
        "advance",
        struct((32, 16, 512)),
        [SMEM] * 3 + [VMEM] * 5,
        VMEM,
        [pltpu.VMEM((16, 768), F32)],
    )(table, a_rate, dt_bias, arrived, carry, x_in, dt_in, b_in)
    own_part, final_state = lax.optimization_barrier((parts[0], final_state))
    mamba_out = call(last_sum_body, "last_sum", struct((2, 4, 512)), [VMEM] * 4, VMEM)(
        own_part, *[along_y(parts[k], k) for k in range(1, 4)]
    )
    return (final_state.reshape(4, 128, 512), mamba_out, attn_out)


def solution(mesh):
    return jax.shard_map(
        per_device,
        mesh=mesh,
        in_specs=(
            P("replica", None, "tensor"),
            P("replica", None, "tensor"),
            P("replica", None, "tensor"),
            P(),
            P(),
            P(None, "replica", "tensor"),
            P(None, "replica", "tensor"),
            P(None, "replica", "tensor"),
            P(None, "replica", None),
            P(None, "replica", None),
            P(None, "replica", "tensor"),
            P(None, "replica", None, "tensor"),
            P("tensor"),
            P("tensor"),
            P("tensor"),
            P("tensor"),
            P("tensor", None),
        ),
        out_specs=(
            P("replica", None, "tensor"),
            P(None, "replica", "tensor"),
            P(None, "replica", "tensor"),
        ),
        check_vma=False,
    )
```

```python
import functools

import jax
import jax.numpy as jnp
from jax import lax
from jax.experimental import pallas as pl
from jax.experimental.pallas import tpu as pltpu
from jax.sharding import PartitionSpec as P

F32 = jnp.float32
BF16 = jnp.bfloat16
HD = 128
STEP_LANES = 1408
CARRY_LANES = 384
ITEM_LANES = STEP_LANES + CARRY_LANES
BACK_LANES = 1536
MASKED = -1e30
MIB = 1024 * 1024

SMEM = pl.BlockSpec(memory_space=pltpu.SMEM)
VMEM = pl.BlockSpec(memory_space=pltpu.VMEM)
HBM = pl.BlockSpec(memory_space=pltpu.HBM)


def call(body, name, out_shape, in_specs, out_specs, scratch=(), flops=1000000, limit=16):
    return pl.pallas_call(
        body,
        name=name,
        out_shape=out_shape,
        in_specs=in_specs,
        out_specs=out_specs,
        scratch_shapes=list(scratch),
        compiler_params=pltpu.CompilerParams(vmem_limit_bytes=int(limit * MIB)),
        cost_estimate=pl.CostEstimate(flops=flops, bytes_accessed=0, transcendentals=0),
    )


def source_of(parents, step, prompt):
    return parents[step, prompt * 4] >> 2


def root_of(parents, prompt):
    return source_of(parents, 0, source_of(parents, 1, prompt))


def fetch(pairs, sems):
    copies = [pltpu.make_async_copy(src, dst, sems.at[i]) for i, (src, dst) in enumerate(pairs)]
    for copy in copies:
        copy.start()
    return copies


def pack_body(*refs):
    sources, item, wide, sems = refs[:6], refs[6], refs[13], refs[14]
    q, kv, c, x, b, dt = refs[7:13]
    copies = fetch(list(zip(sources, refs[7:13])), sems)
    wide[:, STEP_LANES:] = jnp.zeros((8, CARRY_LANES), F32)
    for copy in copies:
        copy.wait()
    for t in range(2):
        rows = pl.ds(4 * t, 4)
        wide[rows, 0:1024] = q[t].astype(F32)
        for s in range(4):
            pair = kv[t, s].astype(F32)
            wide[pl.ds(4 * t + s, 1), 1024:1152] = pair[0:1]
            wide[pl.ds(4 * t + s, 1), 1152:1280] = pair[1:2]
        wide[rows, 1280:1408] = c[t].astype(F32)
    x0 = x[0].astype(F32)
    wide[pl.ds(0, 4), 1408:1792] = x0[:, 0:384]
    wide[pl.ds(4, 4), 1408:1536] = x0[:, 384:512]
    wide[pl.ds(4, 4), 1536:1664] = b[0].astype(F32)
    wide[pl.ds(4, 4), 1664:1672] = dt[0].astype(F32)
    item[...] = wide[...].astype(BF16)


def table_body(parents, lengths, table):
    for slot in range(128):
        table[0, slot] = parents[0, slot]
        table[1, slot] = parents[1, slot]
    for prompt in range(32):
        table[2, source_of(parents, 0, prompt)] = prompt
        table[3, root_of(parents, prompt)] = prompt
        table[4, prompt] = lengths[prompt]


def first_rows(shape):
    return lax.broadcasted_iota(jnp.int32, shape, 0) < 4


def bundle_body(own, up, down, out):
    out[0] = own[...]
    out[1] = up[...]
    out[2] = down[...]


def hold(held, own, up, down):
    for d, (ref, i) in enumerate(
        ((own, 0), (up, 0), (down, 1), (own, 1), (up, 1), (own, 2), (up, 2), (down, 0))
    ):
        held[d] = ref[i]


def stage_quarters_body(source, *refs):
    outs, sems = refs[:4], refs[4]
    pairs = [(source.at[:, pl.ds(1024 * y, 1024)], outs[y]) for y in range(4)]
    for copy in fetch(pairs, sems):
        copy.wait()


def stage_body(*refs):
    half = (len(refs) - 1) // 2
    for copy in fetch(list(zip(refs[:half], refs[half : 2 * half])), refs[-1]):
        copy.wait()


def sort_out_body(table, own, up, down, *refs):
    outs, held = refs[:4], refs[4]
    me = lax.axis_index("replica")
    hold(held, own, up, down)
    first = first_rows((8, STEP_LANES))
    for k in range(4):
        dest = (me + 8 * k) & 31
        for_child = held[(me - table[2, dest]) & 7].astype(F32)
        for_second = held[(me - table[3, dest]) & 7].astype(F32)
        carry = held[(me - source_of(table, 1, dest)) & 7]
        outs[k][:, 0:STEP_LANES] = jnp.where(
            first, for_child[:, 0:STEP_LANES], for_second[:, 0:STEP_LANES]
        ).astype(BF16)
        outs[k][:, STEP_LANES:] = carry[:, STEP_LANES:]


def bundle_back_body(own, one, two, three, out):
    for k, ref in enumerate((own, one, two, three)):
        out[k] = ref[...]


def sort_back_body(parents, own, up, down, *refs):
    outs, held = refs[:3], refs[3]
    me = lax.axis_index("replica")
    held[0], held[1], held[2] = own[...], up[...], down[...]
    first = first_rows((8, BACK_LANES))
    for k, step in enumerate((0, 3, 5)):
        dest = (me & 24) | ((me + step) & 7)

        def pick(source):
            away = (me - source) & 7
            ring = jnp.where(away == 1, 1, jnp.where(away == 7, 2, 0))
            return held[ring, column(me, source)].astype(F32)

        one = pick(source_of(parents, 0, dest))
        two = pick(root_of(parents, dest))
        outs[k][...] = jnp.where(first, one, two).astype(BF16)


def came_by(me, source):
    away = (me - source) & 7
    up = (away >= 2) & (away <= 4)
    down = (away == 5) | (away == 6)
    return jnp.where(up, 1, jnp.where(down, 2, 0))


def column(me, source):
    return ((me >> 3) - (source >> 3)) & 3


def by_row(values, shape):
    row = lax.broadcasted_iota(jnp.int32, shape, 0)
    out = jnp.full(shape, values[-1], jnp.int32)
    for i in range(len(values) - 1):
        out = jnp.where(row == i, values[i], out)
    return out


def nt_dot(a, b):
    return lax.dot_general(a, b, (((1,), (1,)), ((), ())), preferred_element_type=F32)


def attend_body(parents, *refs):
    blocks = refs[:4]
    keys, values, state, back, carry, held = refs[4:10]
    me = lax.axis_index("replica")
    child = parents[2, me]
    second = parents[3, me]
    for k in range(4):
        held[k] = blocks[k][...]
    one = held[column(me, child)].astype(F32)
    two = held[column(me, second)].astype(F32)
    item = jnp.where(first_rows((8, STEP_LANES)), one[:, 0:STEP_LANES], two[:, 0:STEP_LANES])
    carry[...] = held[column(me, source_of(parents, 1, me))][:, STEP_LANES:]

    query = jnp.concatenate([item[:, h * HD : (h + 1) * HD] for h in range(8)], axis=0).astype(BF16)
    pads = jnp.zeros((120, HD), F32)
    new_keys = jnp.concatenate([item[:, 1024:1152], pads], axis=0).astype(BF16)
    new_values = jnp.concatenate([item[:, 1152:1280], pads], axis=0).astype(BF16)
    c_rows = item[:, 1280:1408].astype(BF16)
    ways = [parents[1, second * 4 + s] & 3 for s in range(4)]
    roots = [parents[0, child * 4 + s] & 3 for s in range(4)]
    roots += [parents[0, child * 4 + ways[s]] & 3 for s in range(4)]
    scale = HD ** (-0.5)

    root_rows = by_row(roots, (8, 1024))
    live = lax.broadcasted_iota(jnp.int32, (8, 1024), 1) < parents[4, me]
    scores = jnp.zeros((8, 8, 1024), F32)
    for r in range(4):
        part = nt_dot(query, keys[r]).reshape(8, 8, 1024)
        scores = jnp.where((root_rows == r)[None], part, scores)
    scores = jnp.where(live[None], scores * scale, MASKED)

    row = lax.broadcasted_iota(jnp.int32, (8, HD), 0)
    key_at = lax.broadcasted_iota(jnp.int32, (8, HD), 1)
    way_rows = by_row([0, 1, 2, 3] + ways, (8, HD))
    seen = (key_at == row) | (key_at == way_rows)
    new_scores = nt_dot(query, new_keys).reshape(8, 8, HD) * scale
    new_scores = jnp.where(seen[None], new_scores, MASKED)

    top = jnp.maximum(
        jnp.max(scores, axis=-1, keepdims=True), jnp.max(new_scores, axis=-1, keepdims=True)
    )
    weights = jnp.exp(scores - top)
    new_weights = jnp.exp(new_scores - top)
    total = jnp.sum(weights, axis=-1, keepdims=True) + jnp.sum(new_weights, axis=-1, keepdims=True)
    mixed = jnp.dot(
        new_weights.reshape(64, HD).astype(BF16), new_values, preferred_element_type=F32
    )
    for r in range(4):
        mine = jnp.where((root_rows == r)[None], weights, 0.0).reshape(64, 1024).astype(BF16)
        mixed = mixed + jnp.dot(mine, values[r], preferred_element_type=F32)
    mixed = mixed / total.reshape(64, 1)
    for h in range(8):
        back[:, h * HD : (h + 1) * HD] = mixed[h * 8 : (h + 1) * 8].astype(BF16)

    root_wide = by_row(roots, (8, 512))
    read = jnp.zeros((8, 512), F32)
    for r in range(4):
        part = jnp.dot(c_rows, state[r], preferred_element_type=F32)
        read = jnp.where(root_wide == r, part, read)
    back[:, 1024:1536] = read.astype(BF16)


def per_head(ref, rows=8):
    head = lax.broadcasted_iota(jnp.int32, (rows, 512), 1) >> 6
    out = jnp.full((rows, 512), ref[7], F32)
    for h in range(7):
        out = jnp.where(head == h, ref[h], out)
    return out


def spread_heads(dt):
    head = lax.broadcasted_iota(jnp.int32, (HD, 512), 0)
    lane = lax.broadcasted_iota(jnp.int32, (HD, 512), 1) >> 6
    expand = (head == lane).astype(F32).astype(BF16)
    return jnp.dot(dt.astype(BF16), expand, preferred_element_type=F32)


def step_terms(dt, x, rate, bias):
    raw = spread_heads(dt) + bias
    step = jnp.maximum(raw, 0.0) + jnp.log1p(jnp.exp(-jnp.abs(raw)))
    return jnp.exp(-rate * step), step * x


def parent_rows(parents, me, carry, wide):
    folded = carry.astype(F32)
    wide[pl.ds(8, 4), 0:384] = folded[0:4]
    wide[pl.ds(8, 4), 384:768] = folded[4:8]
    wide[pl.ds(0, 4), :] = jnp.zeros((4, 768), F32)
    for s in range(4):
        way = parents[1, me * 4 + s] & 3
        wide[pl.ds(4 + s, 1), :] = wide[pl.ds(8 + way, 1), :]
    return wide[pl.ds(0, 8), :]


def stacked(ref, wide, lanes):
    wide[pl.ds(0, 4), 0:lanes] = ref[0].astype(F32)
    wide[pl.ds(4, 4), 0:lanes] = ref[1].astype(F32)
    return wide[pl.ds(0, 8), 0:lanes]


def mamba_body(parents, a_rate, dt_bias, skip, *refs):
    blocks = refs[:3]
    carry, x_in, z_in, dt_in, b_in, c_in, gain = refs[3:10]
    proj = refs[10:14]
    attn, keep, send, terms, columns, held, wide = refs[14:21]
    me = lax.axis_index("replica")
    core = lax.axis_index("tensor") & 1
    for k in range(3):
        held[k] = blocks[k][...]
    one = held[came_by(me, source_of(parents, 0, me))].astype(F32)
    two = held[came_by(me, root_of(parents, me))].astype(F32)
    attn[0] = one[0:4, 0:1024].astype(BF16)
    attn[1] = two[4:8, 0:1024].astype(BF16)
    first = first_rows((8, 512))
    read = jnp.where(first, one[:, 1024:BACK_LANES], two[:, 1024:BACK_LANES])

    rate = per_head(a_rate)
    bias = per_head(dt_bias)
    earlier = parent_rows(parents, me, carry[...], wide)
    decay_p, drive_p = step_terms(earlier[:, 640:768], earlier[:, 0:512], rate, bias)
    b_p = earlier[:, 512:640]
    wide[pl.ds(0, 8), 0:HD] = jnp.zeros((8, HD), F32)
    stacked(dt_in, wide, 8)
    dt = wide[pl.ds(0, 8), 0:HD]
    x = stacked(x_in, wide, 512)
    z = stacked(z_in, wide, 512)
    b = stacked(b_in, wide, HD)
    c = stacked(c_in, wide, HD)
    decay, drive = step_terms(dt, x, rate, bias)
    for i, term in enumerate((decay_p, drive_p, decay, drive)):
        terms[i] = term
    columns[0] = jnp.transpose(b_p)
    columns[1] = jnp.transpose(b)
    inner = decay_p * read + drive_p * jnp.sum(b_p * c, axis=-1, keepdims=True)
    inner = jnp.where(first, read, inner)
    out = decay * inner + drive * jnp.sum(b * c, axis=-1, keepdims=True) + per_head(skip) * x
    gated = out * (z / (1.0 + jnp.exp(-z)))
    mean = jnp.mean(gated * gated, axis=-1, keepdims=True)
    normed = (gated * lax.rsqrt(mean + 1e-05) * gain[...]).astype(BF16)
    for y in range(4):
        for target, parity in ((send, 1 - core), (keep, core)):
            span = pl.ds(pl.multiple_of(parity * 512, 512), 512)
            part = jnp.dot(normed, proj[y][:, span], preferred_element_type=F32)
            target[y] = part.astype(BF16)


def core_sum_body(keep, came, *refs):
    outs, total = refs[:4], refs[4]
    y = lax.axis_index("tensor") >> 1
    total[...] = keep[...].astype(F32) + came[...].astype(F32)
    for k in range(4):
        outs[k][...] = total[(y + k) & 3].astype(BF16)


def last_sum_body(a, b, c, d, out):
    total = (a[...].astype(F32) + b[...].astype(F32)) + (c[...].astype(F32) + d[...].astype(F32))
    out[0] = total[0:4].astype(BF16)
    out[1] = total[4:8].astype(BF16)


def regroup_body(parents, came, _, out):
    for prompt in range(32):
        out[prompt] = came[root_of(parents, prompt)]


def advance_body(parents, state, terms, columns, out):
    me = lax.axis_index("replica")
    decay_p, drive_p, decay, drive = [terms[i] for i in range(4)]
    columns_p, columns = columns[0], columns[1]
    source = source_of(parents, 1, me)
    for s in range(4):
        root = parents[0, source * 4 + (parents[1, me * 4 + s] & 3)] & 3
        r = 4 + s
        for i in range(8):
            rows = slice(i * 16, (i + 1) * 16)
            old = state[root * 8 + i].astype(F32)
            mid = decay_p[r : r + 1] * old + drive_p[r : r + 1] * columns_p[rows, r : r + 1]
            mid = mid.astype(BF16).astype(F32)
            new = decay[r : r + 1] * mid + drive[r : r + 1] * columns[rows, r : r + 1]
            out[s * 8 + i] = new.astype(BF16)


def along_x(array, k):
    return lax.ppermute(array, "replica", [(r, ((r + 8 * k) & 31)) for r in range(32)])


def along_z(array, k):
    return lax.ppermute(array, "replica", [(r, (r & 24) | ((r + k) & 7)) for r in range(32)])


def along_y(array, k):
    return lax.ppermute(array, "tensor", [(t, (t + 2 * k) & 7) for t in range(8)])


def across(array):
    return lax.ppermute(array, "tensor", [(t, t ^ 1) for t in range(8)])


def struct(shape, dtype=BF16):
    return jax.ShapeDtypeStruct(shape, dtype)


def per_device(
    ssm_state,
    kcache,
    vcache,
    lengths,
    parents,
    x_in,
    z_in,
    dt_in,
    b_in,
    c_in,
    q_in,
    kv_new,
    a_rate,
    dt_bias,
    skip,
    gain,
    out_proj,
):
    item = call(
        pack_body,
        "pack",
        struct((8, ITEM_LANES)),
        [HBM] * 6,
        VMEM,
        [
            pltpu.VMEM((2, 4, 1024), BF16),
            pltpu.VMEM((2, 4, 2, 128), BF16),
            pltpu.VMEM((2, 4, 128), BF16),
            pltpu.VMEM((2, 4, 512), BF16),
            pltpu.VMEM((2, 4, 128), BF16),
            pltpu.VMEM((2, 4, 8), BF16),
            pltpu.VMEM((8, ITEM_LANES), F32),
            pltpu.SemaphoreType.DMA((6,)),
        ],
        limit=60,
    )(q_in, kv_new, c_in, x_in, b_in, dt_in)
    item, parents = lax.optimization_barrier((item, parents))
    table = call(table_body, "table", struct((8, 128), jnp.int32), [SMEM] * 2, SMEM)(
        parents, lengths
    )
    came_up, came_down = along_z(item, 3), along_z(item, 5)
    item, table, *staged = lax.optimization_barrier((item, table, kcache, vcache, ssm_state))
    bundle = call(
        bundle_body, "bundle", struct((3, 8, ITEM_LANES)), [VMEM] * 3, VMEM
    )(item, came_up, came_down)
    up, down = along_z(bundle, 1), along_z(bundle, 7)
    keys, values, state = call(
        stage_body,
        "stage",
        (struct((4, 1024, 128)), struct((4, 1024, 128)), struct((4, 128, 512))),
        [HBM] * 3,
        (VMEM,) * 3,
        [pltpu.SemaphoreType.DMA((3,))],
    )(*staged)
    bundle, keys, values, state = lax.optimization_barrier((bundle, keys, values, state))
    blocks = call(
        sort_out_body,
        "sort_out",
        (struct((8, ITEM_LANES)),) * 4,
        [SMEM] + [VMEM] * 3,
        (VMEM,) * 4,
        [pltpu.VMEM((8, 8, ITEM_LANES), BF16)],
    )(table, bundle, up, down)
    own_block, moving = lax.optimization_barrier((blocks[0], ssm_state))
    blocks = [own_block] + list(blocks[1:])
    came = lax.all_to_all(moving.reshape(32, 16, 512), "replica", 0, 0, tiled=True)
    blocks = [blocks[0]] + [along_x(blocks[k], k) for k in range(1, 4)]
    back, carry = call(
        attend_body,
        "attend",
        (struct((8, BACK_LANES)), struct((8, CARRY_LANES))),
        [SMEM] + [VMEM] * 7,
        (VMEM,) * 2,
        [pltpu.VMEM((4, 8, ITEM_LANES), BF16)],
        flops=50000000000,
    )(table, *blocks, keys, values, state)
    back, weights = lax.optimization_barrier((back, out_proj))
    weights = call(
        stage_quarters_body,
        "stage_proj",
        (struct((512, 1024)),) * 4,
        [HBM],
        (VMEM,) * 4,
        [pltpu.SemaphoreType.DMA((4,))],
    )(weights)
    others = [along_x(back, k) for k in range(1, 4)]
    back, *weights = lax.optimization_barrier((back, *weights))
    rows = call(
        bundle_back_body, "bundle_back", struct((4, 8, BACK_LANES)), [VMEM] * 4, VMEM
    )(back, *others)
    up, down = along_z(rows, 1), along_z(rows, 7)
    regrouped = call(
        regroup_body, "regroup", struct((32, 16, 512)), [SMEM, VMEM, HBM], VMEM
    )(table, came, rows)
    rows, regrouped = lax.optimization_barrier((rows, regrouped))
    blocks = call(
        sort_back_body,
        "sort_back",
        (struct((8, BACK_LANES)),) * 3,
        [SMEM] + [VMEM] * 3,
        (VMEM,) * 3,
        [pltpu.VMEM((3, 4, 8, BACK_LANES), BF16)],
    )(table, rows, up, down)
    own_block, regrouped = lax.optimization_barrier((blocks[0], regrouped))
    arrived = lax.all_to_all(regrouped, "replica", 0, 0, tiled=True)
    blocks = [own_block, along_z(blocks[1], 3), along_z(blocks[2], 5)]
    attn_out, keep, send, terms, columns = call(
        mamba_body,
        "mamba",
        (
            struct((2, 4, 1024)),
            struct((4, 8, 512)),
            struct((4, 8, 512)),
            struct((4, 8, 512), F32),
            struct((2, 128, 8), F32),
        ),
        [SMEM] * 4 + [VMEM] * 14,
        (VMEM,) * 5,
        [
            pltpu.VMEM((3, 8, BACK_LANES), BF16),
            pltpu.VMEM((16, 768), F32),
        ],
        flops=50000000000,
    )(
        table, a_rate, dt_bias, skip, *blocks, carry, x_in, z_in, dt_in, b_in, c_in,
        gain.reshape(1, 512), *weights,
    )
    parts = call(
        core_sum_body,
        "core_sum",
        (struct((8, 512)),) * 4,
        [VMEM, VMEM],
        (VMEM,) * 4,
        [pltpu.VMEM((4, 8, 512), F32)],
    )(keep, across(send))
    final_state = call(
        advance_body,
        "advance",
        struct((32, 16, 512)),
        [SMEM] + [VMEM] * 3,
        VMEM,
    )(table, arrived, terms, columns)
    own_part, final_state = lax.optimization_barrier((parts[0], final_state))
    mamba_out = call(last_sum_body, "last_sum", struct((2, 4, 512)), [VMEM] * 4, VMEM)(
        own_part, *[along_y(parts[k], k) for k in range(1, 4)]
    )
    return (final_state.reshape(4, 128, 512), mamba_out, attn_out)


def solution(mesh):
    return jax.shard_map(
        per_device,
        mesh=mesh,
        in_specs=(
            P("replica", None, "tensor"),
            P("replica", None, "tensor"),
            P("replica", None, "tensor"),
            P(),
            P(),
            P(None, "replica", "tensor"),
            P(None, "replica", "tensor"),
            P(None, "replica", "tensor"),
            P(None, "replica", None),
            P(None, "replica", None),
            P(None, "replica", "tensor"),
            P(None, "replica", None, "tensor"),
            P("tensor"),
            P("tensor"),
            P("tensor"),
            P("tensor"),
            P("tensor", None),
        ),
        out_specs=(
            P("replica", None, "tensor"),
            P(None, "replica", "tensor"),
            P(None, "replica", "tensor"),
        ),
        check_vma=False,
    )
```
